256 devices in a mesh: dp: 64 (over z_hi, x, y), tensor: 4 (over z_lo, core).
Axes of the slice: x: 4, y: 4, z: 8 (z_hi: 4, z_lo: 2; z = z_hi * 2 + z_lo), core: 2. Of those that a mesh axis runs over, the one named last changes fastest.
Arguments:
- page_acts: bfloat16 [32768, 5120], P('dp', 'tensor'), may hold values from -6 to 6
- out_grad_key: bfloat16 [32768, 1024], P('dp', 'tensor'), may hold values from -6 to 6
- out_grad_value: bfloat16 [32768, 1024], P('dp', 'tensor'), may hold values from -6 to 6
- key_weight: bfloat16 [5120, 1024], P(None, 'tensor'), may hold values from -0.078125 to 0.078125
- value_weight: bfloat16 [5120, 1024], P(None, 'tensor'), may hold values from -0.078125 to 0.078125
Outputs:
- grad_input: bfloat16 [32768, 5120], P('dp', 'tensor')
- fisher_key: float32 [5120, 1024], P('dp', 'tensor')
- fisher_value: float32 [5120, 1024], P('dp', 'tensor')
The draws below stay inside these ranges and needn't reach their ends.
All inputs are finite; a program needn't handle non-finite values.
Results may differ from the reference program's by a relative error of at most 0.001.
Values may be sent and summed in bfloat16 or wider, within the bound.
No kernel may reach another device: no remote copies, remote signals or barrier semaphores. Data moves between devices by JAX's collectives and lax.ppermute only.
A program may use at most 128 MiB of HBM per device.

```python
import jax
import jax.numpy as jnp
from jax import lax

D = 5120
KVW = 1024
PAGE = 512
TOKENS = 32768


def shard_levels(rng, extent, split, least, high):
    def one(position, shards_of):
        heights = jax.random.uniform(jax.random.fold_in(jax.random.fold_in(rng, 6), position), (shards_of,), jnp.float32, least / len(split), high / len(split))
        return jnp.repeat(jnp.exp(heights), extent[position] // shards_of).reshape((-1,) + (1,) * (len(extent) - position - 1))

    loudness = one(*split[0])
    for cut in split[1:]:
        loudness = loudness * one(*cut)
    return loudness


def bell_draw(rng, extent, width, limit, pieces=(), kind=jnp.bfloat16):
    array = width * jax.random.normal(rng, extent, jnp.float32)
    if pieces:
        array = array * shard_levels(rng, extent, pieces, -0.22, 0.18)
    return jnp.clip(array, -limit, limit).astype(kind)


def setup_inputs(seed: int = 0) -> dict:
    seeds = jax.random.split(jax.random.key(seed), 6)
    return {
        "page_acts": bell_draw(seeds[0], (TOKENS, D), 1.0, 6.0, ((0, 64), (1, 4))),
        "out_grad_key": bell_draw(seeds[1], (TOKENS, KVW), 1.0, 6.0, ((0, 64), (1, 4))),
        "out_grad_value": bell_draw(seeds[2], (TOKENS, KVW), 1.0, 6.0, ((0, 64), (1, 4))),
        "key_weight": bell_draw(seeds[3], (D, KVW), D ** -0.5, 0.078125, ((1, 4),)),
        "value_weight": bell_draw(seeds[4], (D, KVW), D ** -0.5, 0.078125, ((1, 4),)),
    }


def reference(page_acts, out_grad_key, out_grad_value, key_weight, value_weight):
    grad_input = (jnp.dot(out_grad_key, key_weight.T, preferred_element_type=jnp.float32)
                  + jnp.dot(out_grad_value, value_weight.T, preferred_element_type=jnp.float32)).astype(jnp.bfloat16)
    count = page_acts.shape[0] // PAGE
    acts = page_acts.reshape(count, PAGE, D)
    keys = out_grad_key.reshape(count, PAGE, KVW)
    values = out_grad_value.reshape(count, PAGE, KVW)

    def accumulate(carry, item):
        act_page, key_page, value_page = item
        key_grad = jnp.dot(act_page.T, key_page, preferred_element_type=jnp.float32)
        value_grad = jnp.dot(act_page.T, value_page, preferred_element_type=jnp.float32)
        return (carry[0] + key_grad * key_grad, carry[1] + value_grad * value_grad), None

    start = (jnp.zeros((D, KVW), jnp.float32), jnp.zeros((D, KVW), jnp.float32))
    totals, _ = lax.scan(accumulate, start, (acts, keys, values))
    factor = 1.0 / (count * PAGE)
    return grad_input, totals[0] * factor, totals[1] * factor
```

```python
import jax
import jax.numpy as jnp
from jax import lax
from jax.experimental import pallas as pl
from jax.experimental.pallas import tpu as pltpu
from jax.sharding import PartitionSpec as P

PAGE = 512
AXES = ("dp", "tensor")
X, Y, ZH, T = 4, 4, 4, 4
BLOCKS = X * Y
ORDER = ((0, 3, 1, 2), (0, 1, 3, 2))
FIRST, SECOND = (1, 3), (3, 1)


def device(zh, x, y, t):
    return (zh * BLOCKS + x * Y + y) * T + t


def devices():
    return [(zh, x, y, t) for zh in range(ZH) for x in range(X) for y in range(Y) for t in range(T)]


def swap(first_axis, distance):
    pairs = []
    for zh, x, y, t in devices():
        along_x = (t % 2 == 0) == first_axis
        there = (x ^ distance, y) if along_x else (x, y ^ distance)
        pairs.append((device(zh, x, y, t), device(zh, *there, t)))
    return pairs


def tensor_swap(flip):
    return [(device(zh, x, y, t), device(zh, x, y, t ^ flip)) for zh, x, y, t in devices()]


def outer_z_swap():
    pairs = []
    for zh, x, y, t in devices():
        z = zh * 2 + t // 2
        there = (z + 1 if z % 2 else z - 1) % (2 * ZH)
        pairs.append((device(zh, x, y, t), device(there // 2, x, y, (there % 2) * 2 + t % 2)))
    return pairs


def owner_step(k):
    return [(device(zh, x, y, t), device(t, x, y, zh ^ k)) for zh, x, y, t in devices()]


def send(value, pairs):
    return lax.ppermute(value, AXES, pairs)


def prepare_kernel(place, a_ref, kw_ref, vw_ref, at0_ref, at1_ref, w0, w1, w2, w3, turned, sems):
    rows = a_ref.shape[1]
    width = kw_ref.shape[1]
    t = place[0]
    copies = []
    for q, out in enumerate((w0, w1, w2, w3)):
        picked = pl.ds(pl.multiple_of((t ^ q) * rows, rows), rows)
        for h, src in enumerate((kw_ref, vw_ref)):
            copies.append(
                pltpu.make_async_copy(
                    src.at[picked, :], out.at[:, pl.ds(h * width, width)], sems.at[2 * q + h]
                )
            )
    for copy in copies:
        copy.start()
    for j in range(0, rows, 128):
        turned[j : j + 128, :] = a_ref[:, j : j + 128].T
    size = rows // BLOCKS
    for s, out in enumerate((at0_ref, at1_ref)):
        for p1 in range(4):
            for p2 in range(4):
                e1, e2 = ORDER[s][p1], ORDER[s][p2]
                block = (place[1] ^ place[4 + e1]) * Y + (place[2] ^ place[8 + e1])
                block = block ^ (place[12 + e2] * Y + place[16 + e2])
                start = pl.multiple_of(block * size, 16)
                to = (p1 * 4 + p2) * size
                out[to : to + size, :] = turned[pl.ds(start, size), :]
    for copy in copies:
        copy.wait()


def prepare(a, kw, vw, place):
    tokens, rows = a.shape
    width = kw.shape[1]
    any_spec = pl.BlockSpec(memory_space=pl.ANY)
    vmem = pl.BlockSpec(memory_space=pltpu.VMEM)
    turned = jax.ShapeDtypeStruct((rows, tokens), a.dtype)
    weights = jax.ShapeDtypeStruct((rows, 2 * width), kw.dtype)
    return pl.pallas_call(
        prepare_kernel,
        in_specs=[pl.BlockSpec(memory_space=pltpu.SMEM), vmem, any_spec, any_spec],
        out_specs=[vmem, vmem] + [any_spec] * 4,
        out_shape=[turned, turned] + [weights] * 4,
        scratch_shapes=[pltpu.VMEM((rows, tokens), a.dtype), pltpu.SemaphoreType.DMA((8,))],
        compiler_params=pltpu.CompilerParams(vmem_limit_bytes=24 << 20),
        cost_estimate=pl.CostEstimate(flops=0, bytes_accessed=16 << 20, transcendentals=0),
    )(place, a, kw, vw)


def squares_kernel(at0, at1, g0, g1, keep0, send0, keep1, send1):
    half = keep0.shape[0]
    width = g0.shape[1] // 2
    step = half // 2
    for at, lo, keep, out in ((at0, 0, keep0, send0), (at1, width, keep1, send1)):
        for dst, base in ((out, half), (keep, 0)):
            for r in range(0, half, step):
                rows = at[base + r : base + r + step, :]
                for h, g in enumerate((g0, g1)):
                    grad = jnp.dot(rows, g[:, lo : lo + width], preferred_element_type=jnp.float32)
                    dst[r : r + step, h * width : (h + 1) * width] = grad * grad


def squares(at0, at1, g0, g1):
    rows, tokens = at0.shape
    width = g0.shape[1]
    half = jax.ShapeDtypeStruct((rows // 2, width), jnp.float32)
    vmem = pl.BlockSpec(memory_space=pltpu.VMEM)
    return pl.pallas_call(
        squares_kernel,
        in_specs=[vmem] * 4,
        out_specs=[vmem] * 4,
        out_shape=[half] * 4,
        compiler_params=pltpu.CompilerParams(vmem_limit_bytes=32 << 20),
        cost_estimate=pl.CostEstimate(
            flops=4 * rows * tokens * width, bytes_accessed=8 << 20, transcendentals=0
        ),
    )(at0, at1, g0, g1)


def right_product(left, right):
    return lax.dot_general(
        left, right, (((1,), (1,)), ((), ())), preferred_element_type=jnp.float32
    )


def per_device(page_acts, out_grad_key, out_grad_value, key_weight, value_weight):
    dp, t = lax.axis_index("dp"), lax.axis_index("tensor")
    zh = dp // BLOCKS
    x, y, core = (dp // Y) % X, dp % Y, t % 2
    e = jnp.arange(4, dtype=jnp.int32)
    none = jnp.zeros((4,), jnp.int32)
    even = core == 0
    place = jnp.concatenate(
        [
            jnp.stack([t, x, y, zh]).astype(jnp.int32),
            jnp.where(even, e, none),
            jnp.where(even, none, e),
            jnp.where(even, none, e),
            jnp.where(even, e, none),
        ]
    )
    width = out_grad_key.shape[1]
    g0 = jnp.concatenate([out_grad_key, out_grad_value], axis=1)
    g2 = send(g0, tensor_swap(2))
    g1 = send(g0, tensor_swap(1))
    at0, at1, w0, w1, w2, w3 = prepare(page_acts, key_weight, value_weight, place)
    w2 = send(w2, outer_z_swap())
    w1 = send(w1, tensor_swap(1))
    g3 = send(g2, tensor_swap(1))
    w3, _ = lax.optimization_barrier((w3, g2))
    w3 = send(w3, tensor_swap(3))

    groups = []
    for near, far in ((g0, g1), (g2, g3)):
        keep0, send0, keep1, send1 = squares(at0, at1, near, far)
        streams = []
        for s, (keep, out) in enumerate(((keep0, send0), (keep1, send1))):
            got = send(out, swap(True, FIRST[s]))
            cut = keep.shape[0] // 2
            out = keep[cut:] + got[cut:]
            kept = keep[:cut] + got[:cut]
            streams.append(kept + send(out, swap(True, SECOND[s])))
        groups.append(streams)

    ends = []
    for s in range(2):
        near, far = groups[0][s], groups[1][s]
        cut = near.shape[0] // 2
        got = send(jnp.stack([near[cut:], far[cut:]]), swap(False, FIRST[s]))
        both = jnp.stack([near[:cut], far[:cut]]) + got
        cut = cut // 2
        got = send(both[:, cut:], swap(False, SECOND[s]))
        ends.append(both[:, :cut] + got)
    size = ends[0].shape[1]
    quarters = jnp.stack(
        [
            jnp.concatenate([part[q // 2, :, (q % 2) * width : (q % 2 + 1) * width] for part in ends], axis=1)
            for q in range(4)
        ]
    )
    total = 0.0
    for k in range(4):
        mine = lax.dynamic_index_in_dim(quarters, t ^ zh ^ k, 0, keepdims=False)
        total = total + send(mine, owner_step(k))
    owned = total * (1.0 / (lax.axis_size("dp") * PAGE))

    grad_input = right_product(g0, w0) + right_product(g1, w1)
    grad_input = grad_input + (right_product(g2, w2) + right_product(g3, w3))
    return grad_input.astype(jnp.bfloat16), owned[:, :width], owned[:, width:]


def solution(mesh):
    in_specs = (
        P("dp", "tensor"),
        P("dp", "tensor"),
        P("dp", "tensor"),
        P(None, "tensor"),
        P(None, "tensor"),
    )
    out_specs = (P("dp", "tensor"), P("dp", "tensor"), P("dp", "tensor"))
    return jax.shard_map(
        per_device, mesh=mesh, in_specs=in_specs, out_specs=out_specs, check_vma=False
    )
```

```python
import functools
import math

import jax
import jax.numpy as jnp
from jax import lax
from jax.experimental import pallas as pl
from jax.experimental.pallas import tpu as pltpu
from jax.sharding import PartitionSpec as P

PAGE = 512
AXES = ("dp", "tensor")
X, Y, ZH, T = 4, 4, 4, 4
BLOCKS = X * Y
ORDER = ((0, 3, 1, 2), (0, 1, 3, 2))
FIRST, SECOND = (1, 3), (3, 1)
HIGH = 16384.0
TAIL = 16
VMEM = pl.BlockSpec(memory_space=pltpu.VMEM)
ANY = pl.BlockSpec(memory_space=pl.ANY)


def device(zh, x, y, t):
    return (zh * BLOCKS + x * Y + y) * T + t


def devices():
    return [(zh, x, y, t) for zh in range(ZH) for x in range(X) for y in range(Y) for t in range(T)]


def swap(first_axis, distance):
    pairs = []
    for zh, x, y, t in devices():
        along_x = (t % 2 == 0) == first_axis
        there = (x ^ distance, y) if along_x else (x, y ^ distance)
        pairs.append((device(zh, x, y, t), device(zh, *there, t)))
    return pairs


def tensor_swap(flip):
    return [(device(zh, x, y, t), device(zh, x, y, t ^ flip)) for zh, x, y, t in devices()]


def outer_z_swap():
    pairs = []
    for zh, x, y, t in devices():
        z = zh * 2 + t // 2
        there = (z + 1 if z % 2 else z - 1) % (2 * ZH)
        pairs.append((device(zh, x, y, t), device(there // 2, x, y, (there % 2) * 2 + t % 2)))
    return pairs


def owner_step(k):
    return [(device(zh, x, y, t), device(t, x, y, zh ^ k)) for zh, x, y, t in devices()]


def send(value, pairs):
    return lax.ppermute(value, AXES, pairs)


def local_call(kernel, out_shape, operands, specs=None, outs=VMEM, scratch=(), flops=0, limit=12):
    moved = sum(math.prod(x.shape) * x.dtype.itemsize for x in (*operands, *out_shape))
    return pl.pallas_call(
        kernel,
        in_specs=specs or [VMEM] * len(operands),
        out_specs=[outs] * len(out_shape),
        out_shape=list(out_shape),
        scratch_shapes=list(scratch),
        compiler_params=pltpu.CompilerParams(vmem_limit_bytes=limit << 20),
        cost_estimate=pl.CostEstimate(flops=flops, bytes_accessed=moved, transcendentals=0),
    )(*operands)


def shape(rows, columns, dtype=jnp.float32):
    return jax.ShapeDtypeStruct((rows, columns), dtype)


def join_kernel(left, right, out, sems):
    width = left.shape[1]
    copies = [
        pltpu.make_async_copy(src, out.at[:, pl.ds(h * width, width)], sems.at[h])
        for h, src in enumerate((left, right))
    ]
    for copy in copies:
        copy.start()
    for copy in copies:
        copy.wait()


def join(left, right):
    rows, width = left.shape
    out = [shape(rows, 2 * width, left.dtype)]
    sems = [pltpu.SemaphoreType.DMA((2,))]
    return local_call(join_kernel, out, (left, right), [ANY] * 2, scratch=sems, limit=2)[0]


def weights_kernel(kw_ref, vw_ref, w0, w1, w2, w3, sems):
    rows, width = w0.shape[0], kw_ref.shape[1]
    t = lax.axis_index("tensor")
    copies = []
    for q, out in ((2, w2), (3, w3), (1, w1), (0, w0)):
        picked = pl.ds(pl.multiple_of((t ^ q) * rows, rows), rows)
        for h, src in enumerate((kw_ref, vw_ref)):
            copies.append(
                pltpu.make_async_copy(
                    src.at[picked, :], out.at[:, pl.ds(h * width, width)], sems.at[2 * q + h]
                )
            )
    for copy in copies:
        copy.start()
    for copy in copies:
        copy.wait()


def pick_weights(kw, vw):
    rows, width = kw.shape[0] // T, kw.shape[1]
    out = [shape(rows, 2 * width, kw.dtype)] * 4
    sems = [pltpu.SemaphoreType.DMA((8,))]
    return local_call(weights_kernel, out, (kw, vw), [ANY] * 2, ANY, sems, limit=2)


def turn_kernel(a_ref, at0_ref, at1_ref, turned):
    rows = a_ref.shape[1]
    dp, t = lax.axis_index("dp"), lax.axis_index("tensor")
    place = dp & (BLOCKS - 1)
    along_x = (t & 1) == 0
    for j in range(0, rows, 128):
        turned[j : j + 128, :] = a_ref[:, j : j + 128].T
    size = rows // BLOCKS
    for s, out in enumerate((at0_ref, at1_ref)):
        for p1 in range(4):
            for p2 in range(4):
                e1, e2 = ORDER[s][p1], ORDER[s][p2]
                block = place ^ jnp.where(along_x, e1 * Y + e2, e2 * Y + e1)
                start = pl.multiple_of(block * size, 16)
                to = (p1 * 4 + p2) * size
                out[to : to + size, :] = turned[pl.ds(start, size), :]


def turn(a):
    tokens, rows = a.shape
    out = [shape(rows, tokens, a.dtype)] * 2
    return local_call(turn_kernel, out, (a,), scratch=[pltpu.VMEM((rows, tokens), a.dtype)])


def exponent_of(bound):
    return jnp.clip(jnp.floor(jnp.log2(HIGH / jnp.maximum(bound, 1e-30))), -60.0, 100.0)


def squares_kernel(at0, at1, g0, g1, keep0, send0, bound0, keep1, send1, bound1):
    half = keep0.shape[0]
    width = g0.shape[1] // 2
    step = half // 2
    streams = ((at0, 0, keep0, send0, bound0), (at1, width, keep1, send1, bound1))
    for at, lo, keep, out, bound in streams:
        for dst, base in ((out, half), (keep, 0)):
            top = jnp.zeros((8, width), jnp.float32)
            for r in range(0, half, step):
                rows = at[base + r : base + r + step, :]
                for h, g in enumerate((g0, g1)):
                    grad = jnp.dot(rows, g[:, lo : lo + width], preferred_element_type=jnp.float32)
                    grad = grad * grad
                    dst[r : r + step, h * width : (h + 1) * width] = grad
                    top = jnp.maximum(top, jnp.max(grad.reshape(-1, 8, width), axis=0))
            top = jnp.max(jnp.max(top, axis=0, keepdims=True), axis=1, keepdims=True)
            top = jnp.broadcast_to(top, bound.shape)
            if dst is keep:
                bound[...] = top
            else:
                exponent = exponent_of(top)
                scale = jnp.exp2(exponent)
                for r in range(0, half, step):
                    out[r : r + step, :] = out[r : r + step, :] * scale
                out[half:, :] = jnp.broadcast_to(exponent, (TAIL, out.shape[1]))


def squares(at0, at1, g0, g1):
    rows, tokens = at0.shape
    width = g0.shape[1]
    half = rows // 2
    out = [shape(half, width), shape(half + TAIL, width), shape(1, width)] * 2
    flops = 4 * rows * tokens * width
    out = local_call(squares_kernel, out, (at0, at1, g0, g1), flops=flops)
    return out[:3], out[3:]


def units_of(got, rows, bound):
    unit = 1.0 / jnp.exp2(got[rows : rows + 1, :])
    return unit, bound[...] + HIGH * unit


def step_kernel(parts, messages, *refs):
    keeps, gots, bounds = refs[:parts], refs[parts : parts + messages], refs[parts + messages :]
    bounds, outs = bounds[:messages], bounds[messages:]
    news, out, new_bound = outs[:parts], outs[parts], outs[parts + 1]
    rows = keeps[0].shape[0]
    half = rows // 2
    each = parts // messages
    scales = [units_of(got, each * rows, bound) for got, bound in zip(gots, bounds)]
    top = functools.reduce(jnp.maximum, [bound for _, bound in scales])
    exponent = exponent_of(top)
    scale = jnp.exp2(exponent)
    new_bound[...] = top
    for i, keep in enumerate(keeps):
        got, unit = gots[i // each], scales[i // each][0]
        base = (i % each) * rows
        for r in range(0, half, 80):
            lo = base + half + r
            more = keep[half + r : half + r + 80, :] + got[lo : lo + 80, :] * unit
            out[i * half + r : i * half + r + 80, :] = more * scale
        for r in range(0, half, 80):
            news[i][r : r + 80, :] = keep[r : r + 80, :] + got[base + r : base + r + 80, :] * unit
    out[parts * half :, :] = jnp.broadcast_to(exponent, (TAIL, out.shape[1]))


def step(keeps, gots, bounds):
    rows, width = keeps[0].shape
    parts, half = len(keeps), rows // 2
    out = [shape(half, width)] * parts + [shape(parts * half + TAIL, width), shape(1, width)]
    kernel = functools.partial(step_kernel, parts, len(gots))
    out = local_call(kernel, out, (*keeps, *gots, *bounds))
    return out[:parts], out[parts], out[parts + 1]


def spread_kernel(near0, far0, got0, bound0, near1, far1, got1, bound1, *refs):
    outs, staged = refs[:T], refs[T]
    rows, width = near0.shape[0], near0.shape[1] // 2
    streams = ((near0, far0, got0, bound0), (near1, far1, got1, bound1))
    for s, (near, far, got, bound) in enumerate(streams):
        unit, top = units_of(got, 2 * rows, bound)
        exponent = exponent_of(top)
        scale = jnp.exp2(exponent)
        base = s * (rows + TAIL)
        tail = jnp.broadcast_to(exponent[:, :width], (TAIL, width))
        for i, keep in enumerate((near, far)):
            value = (keep[...] + got[i * rows : (i + 1) * rows, :] * unit) * scale
            for h in range(2):
                staged[2 * i + h, base : base + rows, :] = value[:, h * width : (h + 1) * width]
                staged[2 * i + h, base + rows : base + rows + TAIL, :] = tail
    distance = lax.axis_index("tensor") ^ (lax.axis_index("dp") >> 4)
    for k, out in enumerate(outs):
        out[...] = staged[distance ^ k]


def spread(operands):
    rows, width = operands[0].shape[0] + TAIL, operands[0].shape[1] // 2
    out = [shape(2 * rows, width)] * T
    return local_call(spread_kernel, out, operands, scratch=[pltpu.VMEM((T, 2 * rows, width), jnp.float32)])


def total_kernel(factor, *refs):
    gots, outs = refs[:-2], refs[-2:]
    rows = outs[0].shape[0]
    for s, out in enumerate(outs):
        base = s * (rows + TAIL)
        total = 0.0
        for got in gots:
            unit = factor / jnp.exp2(got[base + rows : base + rows + 1, :])
            total = total + got[base : base + rows, :] * unit
        out[...] = total


def total(gots, factor):
    rows, width = gots[0].shape[0] // 2 - TAIL, gots[0].shape[1]
    return local_call(functools.partial(total_kernel, factor), [shape(rows, width)] * 2, gots)


def right_product(left, right):
    return lax.dot_general(
        left, right, (((1,), (1,)), ((), ())), preferred_element_type=jnp.float32
    )


def send_narrow(value, pairs):
    return send(value.astype(jnp.float16), pairs).astype(jnp.float32)


def per_device(page_acts, out_grad_key, out_grad_value, key_weight, value_weight):
    g0 = join(out_grad_key, out_grad_value)
    g1 = send(g0, tensor_swap(1))
    g2 = send(g0, tensor_swap(2))
    at0, at1 = turn(page_acts)
    g3 = send(g2, tensor_swap(1))

    near = squares(at0, at1, g0, g1)
    got = [send_narrow(near[s][1], swap(True, FIRST[s])) for s in range(2)]
    kw, vw, _ = lax.optimization_barrier((key_weight, value_weight, near[1][1]))
    w0, w1, w2, w3 = pick_weights(kw, vw)
    kept = [near[s][0] for s in range(2)]
    kept = lax.optimization_barrier((kept, w2, w3))[0]
    w2 = send(w2, outer_z_swap())
    w3, _ = lax.optimization_barrier((w3, g2))
    w3 = send(w3, tensor_swap(3))
    w1 = send(w1, tensor_swap(1))
    far = squares(at0, at1, g2, g3)
    far_got = [send_narrow(far[s][1], swap(True, FIRST[s])) for s in range(2)]
    near = [step([kept[s]], [got[s]], [near[s][2]]) for s in range(2)]
    got = [send_narrow(near[s][1], swap(True, SECOND[s])) for s in range(2)]
    far = [step([far[s][0]], [far_got[s]], [far[s][2]]) for s in range(2)]
    far_got = [send_narrow(far[s][1], swap(True, SECOND[s])) for s in range(2)]

    last = []
    for s in range(2):
        kept = (*near[s][0], *far[s][0])
        kept, out, bound = step(kept, (got[s], far_got[s]), (near[s][2], far[s][2]))
        arrived = send_narrow(out, swap(False, FIRST[s]))
        kept, out, bound = step(kept, [arrived], [bound])
        arrived = send_narrow(out, swap(False, SECOND[s]))
        last += [*kept, arrived, bound]
    outs = spread(last)
    w2, w3, _ = lax.optimization_barrier((w2, w3, outs[0]))
    gots = [send_narrow(out, owner_step(k)) for k, out in enumerate(outs)]
    fisher_key, fisher_value = total(gots, 1.0 / (lax.axis_size("dp") * PAGE))

    grad_input = right_product(g0, w0) + right_product(g1, w1)
    grad_input = grad_input + (right_product(g2, w2) + right_product(g3, w3))
    return grad_input.astype(jnp.bfloat16), fisher_key, fisher_value


def solution(mesh):
    in_specs = (
        P("dp", "tensor"),
        P("dp", "tensor"),
        P("dp", "tensor"),
        P(None, "tensor"),
        P(None, "tensor"),
    )
    out_specs = (P("dp", "tensor"), P("dp", "tensor"), P("dp", "tensor"))
    return jax.shard_map(
        per_device, mesh=mesh, in_specs=in_specs, out_specs=out_specs, check_vma=False
    )
```

```python
import functools

import jax
import jax.numpy as jnp
from jax import lax
from jax.experimental import pallas as pl
from jax.experimental.pallas import tpu as pltpu
from jax.sharding import PartitionSpec as P

PAGE = 512
AXES = ("dp", "tensor")
X, Y, ZH, T = 4, 4, 4, 4
BLOCKS = X * Y
HIGH = 16384.0
TAIL = 16
ORDER = ((0, 3, 1, 2), (0, 1, 3, 2))
FIRST, SECOND = (1, 3), (3, 1)
ADD_COST = 4 << 30
VMEM = pl.BlockSpec(memory_space=pltpu.VMEM)
ANY = pl.BlockSpec(memory_space=pl.ANY)


def device(zh, x, y, t):
    return (zh * BLOCKS + x * Y + y) * T + t


def devices():
    return [(zh, x, y, t) for zh in range(ZH) for x in range(X) for y in range(Y) for t in range(T)]


def swap(first_axis, distance):
    pairs = []
    for zh, x, y, t in devices():
        along_x = (t % 2 == 0) == first_axis
        there = (x ^ distance, y) if along_x else (x, y ^ distance)
        pairs.append((device(zh, x, y, t), device(zh, *there, t)))
    return pairs


def tensor_swap(flip):
    return [(device(zh, x, y, t), device(zh, x, y, t ^ flip)) for zh, x, y, t in devices()]


def z_swap(first):
    pairs = []
    for zh, x, y, t in devices():
        z, core = zh * 2 + t // 2, t % 2
        inner = (core == 1) == first
        there = z ^ 1 if inner else (z + 1 if z % 2 else z - 1) % (2 * ZH)
        to_core = core if first else 1 - core
        pairs.append((device(zh, x, y, t), device(there // 2, x, y, (there % 2) * 2 + to_core)))
    return pairs


def owner_step(k):
    return [(device(zh, x, y, t), device(t, x, y, zh ^ k)) for zh, x, y, t in devices()]


def send(value, pairs):
    return lax.ppermute(value, AXES, pairs)


def local_call(kernel, out_shape, operands, specs=None, outs=VMEM, scratch=(), flops=0, limit=12):
    return pl.pallas_call(
        kernel,
        in_specs=specs or [VMEM] * len(operands),
        out_specs=[outs] * len(out_shape),
        out_shape=list(out_shape),
        scratch_shapes=list(scratch),
        compiler_params=pltpu.CompilerParams(vmem_limit_bytes=limit << 20),
        cost_estimate=pl.CostEstimate(flops=flops, bytes_accessed=0, transcendentals=0),
    )(*operands)


def shape(rows, columns, dtype=jnp.float32):
    return jax.ShapeDtypeStruct((rows, columns), dtype)


def join_kernel(left, right, out, sems):
    width = left.shape[1]
    copies = [
        pltpu.make_async_copy(src, out.at[:, pl.ds(h * width, width)], sems.at[h])
        for h, src in enumerate((left, right))
    ]
    for copy in copies:
        copy.start()
    for copy in copies:
        copy.wait()


def join(left, right):
    rows, width = left.shape
    out = [shape(rows, 2 * width, left.dtype)]
    sems = [pltpu.SemaphoreType.DMA((2,))]
    return local_call(join_kernel, out, (left, right), [ANY] * 2, scratch=sems, limit=2)[0]


def weights_kernel(kw_ref, vw_ref, w0, w1, w2, w3, sems):
    rows, width = w0.shape[0], kw_ref.shape[1]
    t = lax.axis_index("tensor")
    copies = []
    for q, out in ((2, w2), (3, w3), (1, w1), (0, w0)):
        picked = pl.ds(pl.multiple_of((t ^ q) * rows, rows), rows)
        for h, src in enumerate((kw_ref, vw_ref)):
            copies.append(
                pltpu.make_async_copy(
                    src.at[picked, :], out.at[:, pl.ds(h * width, width)], sems.at[2 * q + h]
                )
            )
    for copy in copies:
        copy.start()
    for copy in copies:
        copy.wait()


def pick_weights(kw, vw):
    rows, width = kw.shape[0] // T, kw.shape[1]
    out = [shape(rows, 2 * width, kw.dtype)] * 4
    sems = [pltpu.SemaphoreType.DMA((8,))]
    return local_call(weights_kernel, out, (kw, vw), [ANY] * 2, ANY, sems, limit=2)


def turn_kernel(a_ref, at0_ref, at1_ref, turned):
    rows = a_ref.shape[1]
    dp, t = lax.axis_index("dp"), lax.axis_index("tensor")
    place = dp & (BLOCKS - 1)
    along_x = (t & 1) == 0
    for j in range(0, rows, 128):
        turned[j : j + 128, :] = a_ref[:, j : j + 128].T
    size = rows // BLOCKS
    for out, order in ((at0_ref, ORDER[0]), (at1_ref, ORDER[1])):
        for p1, e1 in enumerate(order):
            for e2 in range(4):
                block = place ^ jnp.where(along_x, e1 * Y + e2, e2 * Y + e1)
                start = pl.multiple_of(block * size, 16)
                to = (p1 * 4 + e2) * size
                out[to : to + size, :] = turned[pl.ds(start, size), :]


def turn(a):
    tokens, rows = a.shape
    out = [shape(rows, tokens, a.dtype)] * 2
    return local_call(turn_kernel, out, (a,), scratch=[pltpu.VMEM((rows, tokens), a.dtype)])


def exponent_of(bound):
    return jnp.clip(jnp.floor(jnp.log2(HIGH / jnp.maximum(bound, 1e-30))), -60.0, 100.0)


def unit_of(exponent):
    return 1.0 / jnp.exp2(exponent)


def fill(out, at, count, row):
    out[at : at + count, :] = jnp.broadcast_to(row, (count, out.shape[1]))


def squares_kernel(at0, at1, g0, g1, keep0, bound0, out0, keep1, bound1, out1):
    half, width = keep0.shape[0], g0.shape[1] // 2
    step = half // 2
    streams = ((at0, 0, keep0, bound0, out0), (at1, width, keep1, bound1, out1))
    for moved in (True, False):
        for at, lo, keep, bound, out in streams:
            tops = [jnp.zeros((8, width), jnp.float32)] * 2
            to, base = (out, half) if moved else (keep, 0)
            for r in range(0, half, step):
                rows = at[base + r : base + r + step, :]
                for h, g in enumerate((g0, g1)):
                    grad = jnp.dot(rows, g[:, lo : lo + width], preferred_element_type=jnp.float32)
                    grad = grad * grad
                    to[r : r + step, h * width : (h + 1) * width] = grad
                    tops[h] = jnp.maximum(tops[h], jnp.max(grad.reshape(-1, 8, width), axis=0))
            top = jnp.concatenate([jnp.max(top, axis=0, keepdims=True) for top in tops], axis=1)
            if moved:
                exponent = exponent_of(top)
                scale = jnp.exp2(exponent)
                for r in range(0, half, 80):
                    out[r : r + 80, :] = out[r : r + 80, :] * scale
                fill(out, half, TAIL, exponent)
            else:
                bound[...] = top


def squares(at0, at1, g0, g1):
    rows, width = at0.shape[0], g0.shape[1]
    out = [shape(rows // 2, width), shape(1, width), shape(rows // 2 + TAIL, width)] * 2
    out = local_call(squares_kernel, out, (at0, at1, g0, g1))
    return out[:3], out[3:]


def add_kernel(keep0, bound0, got0, keep1, bound1, got1, sum0, top0, sum1, top1):
    rows = keep0.shape[0]
    for keep, bound, got, total, top in (
        (keep0, bound0, got0, sum0, top0),
        (keep1, bound1, got1, sum1, top1),
    ):
        unit = unit_of(got[rows : rows + 1, :])
        top[...] = bound[...] + HIGH * unit
        for r in range(0, rows, 80):
            total[r : r + 80, :] = keep[r : r + 80, :] + got[r : r + 80, :] * unit


def add(*operands):
    rows, width = operands[0].shape
    out = local_call(add_kernel, [shape(rows, width), shape(1, width)] * 2, operands, flops=ADD_COST)
    return out[:2], out[2:]


def halve_kernel(near, near_bound, keep, bound, got, new0, new1, bounds, out):
    rows = keep.shape[0]
    half = rows // 2
    unit = unit_of(got[rows : rows + 1, :])
    tops = (near_bound[...], bound[...] + HIGH * unit)
    exponents = [exponent_of(top) for top in tops]
    scales = [jnp.exp2(exponent) for exponent in exponents]
    for r in range(half, rows, 80):
        to = r - half
        out[to : to + 80, :] = near[r : r + 80, :] * scales[0]
        value = keep[r : r + 80, :] + got[r : r + 80, :] * unit
        out[r : r + 80, :] = value * scales[1]
    for r in range(0, half, 80):
        new0[r : r + 80, :] = near[r : r + 80, :]
        new1[r : r + 80, :] = keep[r : r + 80, :] + got[r : r + 80, :] * unit
    for h in range(2):
        bounds[h : h + 1, :] = tops[h]
        fill(out, rows + h * (TAIL // 2), TAIL // 2, exponents[h])


def halve(*operands):
    rows, width = operands[0].shape
    out = [shape(rows // 2, width)] * 2 + [shape(2, width), shape(rows + TAIL, width)]
    return local_call(halve_kernel, out, operands)


def share_kernel(near0, far0, bounds0, got0, near1, far1, bounds1, got1, own, bounds, *outs):
    rows = near0.shape[0]
    size, each = rows // 4, TAIL // 4
    streams = ((near0, far0, bounds0, got0), (near1, far1, bounds1, got1))
    for s, (near, far, kept_bounds, got) in enumerate(streams):
        for h, keep in enumerate((near, far)):
            p = 2 * s + h
            tail = 2 * rows + h * (TAIL // 2)
            unit = unit_of(got[tail : tail + 1, :])
            top = kept_bounds[h : h + 1, :] + HIGH * unit
            exponent = exponent_of(top)
            scale = jnp.exp2(exponent)
            bounds[p : p + 1, :] = top
            for e, out in ((1, outs[0]), (3, outs[2]), (2, outs[1]), (0, own)):
                at = e * size
                arrived = got[h * rows + at : h * rows + at + size, :]
                value = keep[at : at + size, :] + arrived * unit
                out[p * size : (p + 1) * size, :] = value if e == 0 else value * scale
            for out in outs:
                fill(out, 4 * size + p * each, each, exponent)


def share(*operands):
    rows, width = operands[0].shape
    out = [shape(rows, width), shape(4, width)] + [shape(rows + TAIL, width)] * 3
    own, bounds, *messages = local_call(share_kernel, out, operands)
    return own, bounds, messages


def spread_kernel(own, bounds, got1, got2, got3, *refs):
    outs, staged = refs[:T], refs[T]
    rows, width = own.shape[0], own.shape[1] // 2
    size = rows // 4
    for p in range(4):
        tail = rows + p * (TAIL // 4)
        value, top = own[p * size : (p + 1) * size, :], bounds[p : p + 1, :]
        for got in (got1, got2, got3):
            unit = unit_of(got[tail : tail + 1, :])
            value = value + got[p * size : (p + 1) * size, :] * unit
            top = top + HIGH * unit
        exponent = exponent_of(top)
        value = value * jnp.exp2(exponent)
        s, h = p // 2, p % 2
        for i in range(2):
            q, columns = 2 * h + i, slice(i * width, (i + 1) * width)
            staged[q, s * size : (s + 1) * size, :] = value[:, columns]
            row = jnp.broadcast_to(exponent[:, columns], (TAIL // 2, width))
            to = 2 * size + s * (TAIL // 2)
            staged[q, to : to + TAIL // 2, :] = row
    distance = lax.axis_index("tensor") ^ (lax.axis_index("dp") >> 4)
    for k, out in enumerate(outs):
        out[...] = staged[distance ^ k]


def spread(*operands):
    rows, width = operands[0].shape[0] // 2 + TAIL, operands[0].shape[1] // 2
    scratch = [pltpu.VMEM((T, rows, width), jnp.float32)]
    return local_call(spread_kernel, [shape(rows, width)] * T, operands, scratch=scratch)


def total_kernel(factor, *refs):
    gots, outs = refs[:-2], refs[-2:]
    size = outs[0].shape[0]
    for s, out in enumerate(outs):
        tail = 2 * size + s * (TAIL // 2)
        total = 0.0
        for got in gots:
            unit = factor / jnp.exp2(got[tail : tail + 1, :])
            total = total + got[s * size : (s + 1) * size, :] * unit
        out[...] = total


def total(gots, factor):
    rows, width = (gots[0].shape[0] - TAIL) // 2, gots[0].shape[1]
    return local_call(functools.partial(total_kernel, factor), [shape(rows, width)] * 2, gots)


def right_product(left, right):
    return lax.dot_general(
        left, right, (((1,), (1,)), ((), ())), preferred_element_type=jnp.float32
    )


def narrow(values):
    return [value.astype(jnp.float16) for value in values]


def wide(values):
    return [value.astype(jnp.float32) for value in values]


def per_device(page_acts, out_grad_key, out_grad_value, key_weight, value_weight):
    g0 = join(out_grad_key, out_grad_value)
    g2 = send(g0, tensor_swap(2))
    g1 = send(g0, tensor_swap(1))
    at = turn(page_acts)

    near = squares(*at, g0, g1)
    out = narrow([stream[2] for stream in near])
    near_got = wide([send(out[s], swap(True, FIRST[s])) for s in range(2)])
    kw, vw, _ = lax.optimization_barrier((key_weight, value_weight, out))
    w0, w1, w2, w3 = pick_weights(kw, vw)
    g2, _ = lax.optimization_barrier((g2, w2))
    g3 = send(g2, tensor_swap(1))
    w2 = send(w2, z_swap(True))
    near = add(*near[0][:2], near_got[0], *near[1][:2], near_got[1])
    far = squares(*at, g2, g3)
    out = narrow([stream[2] for stream in far])
    out, near, w3 = lax.optimization_barrier((out, near, w3))
    far_got = [send(out[s], swap(True, FIRST[s])) for s in range(2)]
    w2, w3 = lax.optimization_barrier((w2, w3))
    w3 = send(w3, z_swap(False))
    far_got = wide(far_got)

    streams = [halve(*near[s], *far[s][:2], far_got[s]) for s in range(2)]
    out = narrow([stream[3] for stream in streams])
    out, w1 = lax.optimization_barrier((out, w1))
    got = [send(out[s], swap(True, SECOND[s])) for s in range(2)]
    w1 = send(w1, tensor_swap(1))
    got, w3 = lax.optimization_barrier((got, w3))
    got = wide(got)
    own, bounds, out = share(*streams[0][:3], got[0], *streams[1][:3], got[1])
    got = [send(part, swap(False, e + 1)) for e, part in enumerate(narrow(out))]
    got, w1 = lax.optimization_barrier((got, w1))
    outs = spread(own, bounds, *wide(got))
    w1, w2, w3, _ = lax.optimization_barrier((w1, w2, w3, outs))
    got = [send(out, owner_step(k)) for k, out in enumerate(narrow(outs))]
    fisher_key, fisher_value = total(wide(got), 1.0 / (lax.axis_size("dp") * PAGE))

    grad_input = right_product(g0, w0) + right_product(g1, w1)
    grad_input = grad_input + (right_product(g2, w2) + right_product(g3, w3))
    return grad_input.astype(jnp.bfloat16), fisher_key, fisher_value


def solution(mesh):
    in_specs = (
        P("dp", "tensor"),
        P("dp", "tensor"),
        P("dp", "tensor"),
        P(None, "tensor"),
        P(None, "tensor"),
    )
    out_specs = (P("dp", "tensor"), P("dp", "tensor"), P("dp", "tensor"))
    return jax.shard_map(
        per_device, mesh=mesh, in_specs=in_specs, out_specs=out_specs, check_vma=False
    )
```

```python
import functools

import jax
import jax.numpy as jnp
from jax import lax
from jax.experimental import pallas as pl
from jax.experimental.pallas import tpu as pltpu
from jax.sharding import PartitionSpec as P

PAGE = 512
AXES = ("dp", "tensor")
X, Y, ZH, T = 4, 4, 4, 4
BLOCKS = X * Y
HIGH = 16384.0
TAIL = 16
ORDER = ((0, 3, 1, 2), (0, 1, 3, 2))
FIRST, SECOND = (1, 3), (3, 1)
ADD_COST = 4 << 30
VMEM = pl.BlockSpec(memory_space=pltpu.VMEM)
ANY = pl.BlockSpec(memory_space=pl.ANY)


def device(zh, x, y, t):
    return (zh * BLOCKS + x * Y + y) * T + t


def devices():
    return [(zh, x, y, t) for zh in range(ZH) for x in range(X) for y in range(Y) for t in range(T)]


def swap(first_axis, distance):
    pairs = []
    for zh, x, y, t in devices():
        along_x = (t % 2 == 0) == first_axis
        there = (x ^ distance, y) if along_x else (x, y ^ distance)
        pairs.append((device(zh, x, y, t), device(zh, *there, t)))
    return pairs


def tensor_swap(flip):
    return [(device(zh, x, y, t), device(zh, x, y, t ^ flip)) for zh, x, y, t in devices()]


def outer_z_swap():
    pairs = []
    for zh, x, y, t in devices():
        z = zh * 2 + t // 2
        there = (z + 1 if z % 2 else z - 1) % (2 * ZH)
        pairs.append((device(zh, x, y, t), device(there // 2, x, y, (there % 2) * 2 + t % 2)))
    return pairs


def owner_step(k):
    return [(device(zh, x, y, t), device(t, x, y, zh ^ k)) for zh, x, y, t in devices()]


def send(value, pairs):
    return lax.ppermute(value, AXES, pairs)


def local_call(kernel, out_shape, operands, specs=None, outs=VMEM, scratch=(), flops=0, limit=12):
    return pl.pallas_call(
        kernel,
        in_specs=specs or [VMEM] * len(operands),
        out_specs=[outs] * len(out_shape),
        out_shape=list(out_shape),
        scratch_shapes=list(scratch),
        compiler_params=pltpu.CompilerParams(vmem_limit_bytes=limit << 20),
        cost_estimate=pl.CostEstimate(flops=flops, bytes_accessed=0, transcendentals=0),
    )(*operands)


def shape(rows, columns, dtype=jnp.float32):
    return jax.ShapeDtypeStruct((rows, columns), dtype)


def join_kernel(left, right, out, sems):
    width = left.shape[1]
    copies = [
        pltpu.make_async_copy(src, out.at[:, pl.ds(h * width, width)], sems.at[h])
        for h, src in enumerate((left, right))
    ]
    for copy in copies:
        copy.start()
    for copy in copies:
        copy.wait()


def join(left, right):
    rows, width = left.shape
    out = [shape(rows, 2 * width, left.dtype)]
    sems = [pltpu.SemaphoreType.DMA((2,))]
    return local_call(join_kernel, out, (left, right), [ANY] * 2, scratch=sems, limit=2)[0]


def weights_kernel(kw_ref, vw_ref, w0, w1, w2, w3, sems):
    rows, width = w0.shape[0], kw_ref.shape[1]
    t = lax.axis_index("tensor")
    copies = []
    for q, out in ((2, w2), (3, w3), (1, w1), (0, w0)):
        picked = pl.ds(pl.multiple_of((t ^ q) * rows, rows), rows)
        for h, src in enumerate((kw_ref, vw_ref)):
            copies.append(
                pltpu.make_async_copy(
                    src.at[picked, :], out.at[:, pl.ds(h * width, width)], sems.at[2 * q + h]
                )
            )
    for copy in copies:
        copy.start()
    for copy in copies:
        copy.wait()


def pick_weights(kw, vw):
    rows, width = kw.shape[0] // T, kw.shape[1]
    out = [shape(rows, 2 * width, kw.dtype)] * 4
    sems = [pltpu.SemaphoreType.DMA((8,))]
    return local_call(weights_kernel, out, (kw, vw), [ANY] * 2, ANY, sems, limit=2)


def turn_kernel(a_ref, at0_ref, at1_ref, turned):
    rows = a_ref.shape[1]
    dp, t = lax.axis_index("dp"), lax.axis_index("tensor")
    place = dp & (BLOCKS - 1)
    along_x = (t & 1) == 0
    for j in range(0, rows, 128):
        turned[j : j + 128, :] = a_ref[:, j : j + 128].T
    size = rows // BLOCKS
    for out, order in ((at0_ref, ORDER[0]), (at1_ref, ORDER[1])):
        for p1, e1 in enumerate(order):
            for e2 in range(4):
                block = place ^ jnp.where(along_x, e1 * Y + e2, e2 * Y + e1)
                start = pl.multiple_of(block * size, 16)
                to = (p1 * 4 + e2) * size
                out[to : to + size, :] = turned[pl.ds(start, size), :]


def turn(a):
    tokens, rows = a.shape
    out = [shape(rows, tokens, a.dtype)] * 2
    return local_call(turn_kernel, out, (a,), scratch=[pltpu.VMEM((rows, tokens), a.dtype)])


def exponent_of(bound):
    return jnp.clip(jnp.floor(jnp.log2(HIGH / jnp.maximum(bound, 1e-30))), -60.0, 100.0)


def unit_of(exponent):
    return 1.0 / jnp.exp2(exponent)


def fill(out, at, count, row):
    out[at : at + count, :] = jnp.broadcast_to(row, (count, out.shape[1]))


def squares_kernel(at0, at1, g0, g1, keep0, bound0, out0, keep1, bound1, out1):
    half, width = keep0.shape[0], g0.shape[1] // 2
    step = half // 2
    streams = ((at0, 0, keep0, bound0, out0), (at1, width, keep1, bound1, out1))
    for moved in (True, False):
        for at, lo, keep, bound, out in streams:
            tops = [jnp.zeros((8, width), jnp.float32)] * 2
            to, base = (out, half) if moved else (keep, 0)
            for r in range(0, half, step):
                rows = at[base + r : base + r + step, :]
                for h, g in enumerate((g0, g1)):
                    grad = jnp.dot(rows, g[:, lo : lo + width], preferred_element_type=jnp.float32)
                    grad = grad * grad
                    to[r : r + step, h * width : (h + 1) * width] = grad
                    tops[h] = jnp.maximum(tops[h], jnp.max(grad.reshape(-1, 8, width), axis=0))
            top = jnp.concatenate([jnp.max(top, axis=0, keepdims=True) for top in tops], axis=1)
            if moved:
                exponent = exponent_of(top)
                scale = jnp.exp2(exponent)
                for r in range(0, half, 80):
                    out[r : r + 80, :] = out[r : r + 80, :] * scale
                fill(out, half, TAIL, exponent)
            else:
                bound[...] = top


def squares(at0, at1, g0, g1):
    rows, width = at0.shape[0], g0.shape[1]
    out = [shape(rows // 2, width), shape(1, width), shape(rows // 2 + TAIL, width)] * 2
    out = local_call(squares_kernel, out, (at0, at1, g0, g1))
    return out[:3], out[3:]


def add_kernel(keep0, bound0, got0, keep1, bound1, got1, sum0, top0, sum1, top1):
    rows = keep0.shape[0]
    for keep, bound, got, total, top in (
        (keep0, bound0, got0, sum0, top0),
        (keep1, bound1, got1, sum1, top1),
    ):
        unit = unit_of(got[rows : rows + 1, :])
        top[...] = bound[...] + HIGH * unit
        for r in range(0, rows, 80):
            total[r : r + 80, :] = keep[r : r + 80, :] + got[r : r + 80, :] * unit


def add(*operands):
    rows, width = operands[0].shape
    out = local_call(add_kernel, [shape(rows, width), shape(1, width)] * 2, operands, flops=ADD_COST)
    return out[:2], out[2:]


def halve_kernel(near, near_bound, keep, bound, got, new0, new1, bounds, out):
    rows = keep.shape[0]
    half = rows // 2
    unit = unit_of(got[rows : rows + 1, :])
    tops = (near_bound[...], bound[...] + HIGH * unit)
    exponents = [exponent_of(top) for top in tops]
    scales = [jnp.exp2(exponent) for exponent in exponents]
    for r in range(half, rows, 80):
        to = r - half
        out[to : to + 80, :] = near[r : r + 80, :] * scales[0]
        value = keep[r : r + 80, :] + got[r : r + 80, :] * unit
        out[r : r + 80, :] = value * scales[1]
    for r in range(0, half, 80):
        new0[r : r + 80, :] = near[r : r + 80, :]
        new1[r : r + 80, :] = keep[r : r + 80, :] + got[r : r + 80, :] * unit
    for h in range(2):
        bounds[h : h + 1, :] = tops[h]
        fill(out, rows + h * (TAIL // 2), TAIL // 2, exponents[h])


def halve(*operands):
    rows, width = operands[0].shape
    out = [shape(rows // 2, width)] * 2 + [shape(2, width), shape(rows + TAIL, width)]
    return local_call(halve_kernel, out, operands)


def share_kernel(near0, far0, bounds0, got0, near1, far1, bounds1, got1, own, bounds, *outs):
    rows = near0.shape[0]
    size, each = rows // 4, TAIL // 4
    streams = ((near0, far0, bounds0, got0), (near1, far1, bounds1, got1))
    for s, (near, far, kept_bounds, got) in enumerate(streams):
        for h, keep in enumerate((near, far)):
            p = 2 * s + h
            tail = 2 * rows + h * (TAIL // 2)
            unit = unit_of(got[tail : tail + 1, :])
            top = kept_bounds[h : h + 1, :] + HIGH * unit
            exponent = exponent_of(top)
            scale = jnp.exp2(exponent)
            bounds[p : p + 1, :] = top
            for e, out in ((1, outs[0]), (3, outs[2]), (2, outs[1]), (0, own)):
                at = e * size
                arrived = got[h * rows + at : h * rows + at + size, :]
                value = keep[at : at + size, :] + arrived * unit
                out[p * size : (p + 1) * size, :] = value if e == 0 else value * scale
            for out in outs:
                fill(out, 4 * size + p * each, each, exponent)


def share(*operands):
    rows, width = operands[0].shape
    out = [shape(rows, width), shape(4, width)] + [shape(rows + TAIL, width)] * 3
    own, bounds, *messages = local_call(share_kernel, out, operands)
    return own, bounds, messages


def spread_kernel(own, bounds, got1, got2, got3, *refs):
    outs, staged = refs[:T], refs[T]
    rows, width = own.shape[0], own.shape[1] // 2
    size = rows // 4
    for p in range(4):
        tail = rows + p * (TAIL // 4)
        value, top = own[p * size : (p + 1) * size, :], bounds[p : p + 1, :]
        for got in (got1, got2, got3):
            unit = unit_of(got[tail : tail + 1, :])
            value = value + got[p * size : (p + 1) * size, :] * unit
            top = top + HIGH * unit
        exponent = exponent_of(top)
        value = value * jnp.exp2(exponent)
        s, h = p // 2, p % 2
        for i in range(2):
            q, columns = 2 * h + i, slice(i * width, (i + 1) * width)
            staged[q, s * size : (s + 1) * size, :] = value[:, columns]
            row = jnp.broadcast_to(exponent[:, columns], (TAIL // 2, width))
            to = 2 * size + s * (TAIL // 2)
            staged[q, to : to + TAIL // 2, :] = row
    distance = lax.axis_index("tensor") ^ (lax.axis_index("dp") >> 4)
    for k, out in enumerate(outs):
        out[...] = staged[distance ^ k]


def spread(*operands):
    rows, width = operands[0].shape[0] // 2 + TAIL, operands[0].shape[1] // 2
    scratch = [pltpu.VMEM((T, rows, width), jnp.float32)]
    return local_call(spread_kernel, [shape(rows, width)] * T, operands, scratch=scratch)


def total_kernel(factor, *refs):
    gots, outs = refs[:-2], refs[-2:]
    size = outs[0].shape[0]
    for s, out in enumerate(outs):
        tail = 2 * size + s * (TAIL // 2)
        total = 0.0
        for got in gots:
            unit = factor / jnp.exp2(got[tail : tail + 1, :])
            total = total + got[s * size : (s + 1) * size, :] * unit
        out[...] = total


def total(gots, factor):
    rows, width = (gots[0].shape[0] - TAIL) // 2, gots[0].shape[1]
    return local_call(functools.partial(total_kernel, factor), [shape(rows, width)] * 2, gots)


def right_product(left, right):
    return lax.dot_general(
        left, right, (((1,), (1,)), ((), ())), preferred_element_type=jnp.float32
    )


def narrow(values):
    return [value.astype(jnp.float16) for value in values]


def wide(values):
    return [value.astype(jnp.float32) for value in values]


def per_device(page_acts, out_grad_key, out_grad_value, key_weight, value_weight):
    g0 = join(out_grad_key, out_grad_value)
    g2 = send(g0, tensor_swap(2))
    g1 = send(g0, tensor_swap(1))
    at = turn(page_acts)

    near = squares(*at, g0, g1)
    out = narrow([stream[2] for stream in near])
    near_got = wide([send(out[s], swap(True, FIRST[s])) for s in range(2)])
    kw, vw, _ = lax.optimization_barrier((key_weight, value_weight, out))
    w0, w1, w2, w3 = pick_weights(kw, vw)
    g2, _ = lax.optimization_barrier((g2, w2))
    g3 = send(g2, tensor_swap(1))
    near = add(*near[0][:2], near_got[0], *near[1][:2], near_got[1])
    far = squares(*at, g2, g3)
    out = narrow([stream[2] for stream in far])
    out, near, w2, w3 = lax.optimization_barrier((out, near, w2, w3))
    far_got = [send(out[s], swap(True, FIRST[s])) for s in range(2)]
    w1 = send(w1, tensor_swap(1))
    w1, w2, w3 = lax.optimization_barrier((w1, w2, w3))
    w2 = send(w2, outer_z_swap())
    w3 = send(w3, tensor_swap(3))
    far_got = wide(far_got)

    streams = [halve(*near[s], *far[s][:2], far_got[s]) for s in range(2)]
    out = narrow([stream[3] for stream in streams])
    got = [send(out[s], swap(True, SECOND[s])) for s in range(2)]
    grad_input = right_product(g0, w0) + right_product(g1, w1)
    got, grad_input = lax.optimization_barrier((wide(got), grad_input))
    own, bounds, out = share(*streams[0][:3], got[0], *streams[1][:3], got[1])
    out = narrow(out)
    one, three, two = (send(out[e - 1], swap(False, e)) for e in (1, 3, 2))
    got = [one, two, three]
    got, w2, w3 = lax.optimization_barrier((wide(got), w2, w3))
    outs = spread(own, bounds, *got)
    w1, w2, w3, _ = lax.optimization_barrier((w1, w2, w3, outs))
    got = [send(out, owner_step(k)) for k, out in enumerate(narrow(outs))]
    fisher_key, fisher_value = total(wide(got), 1.0 / (lax.axis_size("dp") * PAGE))

    grad_input = grad_input + (right_product(g2, w2) + right_product(g3, w3))
    return grad_input.astype(jnp.bfloat16), fisher_key, fisher_value


def solution(mesh):
    in_specs = (
        P("dp", "tensor"),
        P("dp", "tensor"),
        P("dp", "tensor"),
        P(None, "tensor"),
        P(None, "tensor"),
    )
    out_specs = (P("dp", "tensor"), P("dp", "tensor"), P("dp", "tensor"))
    return jax.shard_map(
        per_device, mesh=mesh, in_specs=in_specs, out_specs=out_specs, check_vma=False
    )
```

```python
import functools

import jax
import jax.numpy as jnp
from jax import lax
from jax.experimental import pallas as pl
from jax.experimental.pallas import tpu as pltpu
from jax.sharding import PartitionSpec as P

PAGE = 512
AXES = ("dp", "tensor")
X, Y, ZH, T = 4, 4, 4, 4
BLOCKS = X * Y
HIGH = 16384.0
TAIL = 16
ORDER = ((0, 3, 1, 2), (0, 1, 3, 2))
FIRST, SECOND = (1, 3), (3, 1)
ADD_COST = 4 << 30
VMEM = pl.BlockSpec(memory_space=pltpu.VMEM)
ANY = pl.BlockSpec(memory_space=pl.ANY)


def device(zh, x, y, t):
    return (zh * BLOCKS + x * Y + y) * T + t


def devices():
    return [(zh, x, y, t) for zh in range(ZH) for x in range(X) for y in range(Y) for t in range(T)]


def swap(first_axis, distance):
    pairs = []
    for zh, x, y, t in devices():
        along_x = (t % 2 == 0) == first_axis
        there = (x ^ distance, y) if along_x else (x, y ^ distance)
        pairs.append((device(zh, x, y, t), device(zh, *there, t)))
    return pairs


def tensor_swap(flip):
    return [(device(zh, x, y, t), device(zh, x, y, t ^ flip)) for zh, x, y, t in devices()]


def outer_z_swap():
    pairs = []
    for zh, x, y, t in devices():
        z = zh * 2 + t // 2
        there = (z + 1 if z % 2 else z - 1) % (2 * ZH)
        pairs.append((device(zh, x, y, t), device(there // 2, x, y, (there % 2) * 2 + t % 2)))
    return pairs


def owner_step(k):
    return [(device(zh, x, y, t), device(t, x, y, zh ^ k)) for zh, x, y, t in devices()]


def send(value, pairs):
    return lax.ppermute(value, AXES, pairs)


def local_call(kernel, out_shape, operands, specs=None, outs=VMEM, scratch=(), flops=0, limit=12):
    return pl.pallas_call(
        kernel,
        in_specs=specs or [VMEM] * len(operands),
        out_specs=[outs] * len(out_shape),
        out_shape=list(out_shape),
        scratch_shapes=list(scratch),
        compiler_params=pltpu.CompilerParams(vmem_limit_bytes=limit << 20),
        cost_estimate=pl.CostEstimate(flops=flops, bytes_accessed=0, transcendentals=0),
    )(*operands)


def shape(rows, columns, dtype=jnp.float32):
    return jax.ShapeDtypeStruct((rows, columns), dtype)


def join_kernel(left, right, out, sems):
    width = left.shape[1]
    copies = [
        pltpu.make_async_copy(src, out.at[:, pl.ds(h * width, width)], sems.at[h])
        for h, src in enumerate((left, right))
    ]
    for copy in copies:
        copy.start()
    for copy in copies:
        copy.wait()


def join(left, right):
    rows, width = left.shape
    out = [shape(rows, 2 * width, left.dtype)]
    sems = [pltpu.SemaphoreType.DMA((2,))]
    return local_call(join_kernel, out, (left, right), [ANY] * 2, scratch=sems, limit=2)[0]


def weights_kernel(kw_ref, vw_ref, w0, w1, w2, w3, sems):
    rows, width = w0.shape[0], kw_ref.shape[1]
    t = lax.axis_index("tensor")
    copies = []
    for q, out in ((2, w2), (3, w3), (1, w1), (0, w0)):
        picked = pl.ds(pl.multiple_of((t ^ q) * rows, rows), rows)
        for h, src in enumerate((kw_ref, vw_ref)):
            copies.append(
                pltpu.make_async_copy(
                    src.at[picked, :], out.at[:, pl.ds(h * width, width)], sems.at[2 * q + h]
                )
            )
    for copy in copies:
        copy.start()
    for copy in copies:
        copy.wait()


def pick_weights(kw, vw):
    rows, width = kw.shape[0] // T, kw.shape[1]
    out = [shape(rows, 2 * width, kw.dtype)] * 4
    sems = [pltpu.SemaphoreType.DMA((8,))]
    return local_call(weights_kernel, out, (kw, vw), [ANY] * 2, ANY, sems, limit=2)


def turn_kernel(a_ref, at0_ref, at1_ref, turned):
    rows = a_ref.shape[1]
    dp, t = lax.axis_index("dp"), lax.axis_index("tensor")
    place = dp & (BLOCKS - 1)
    along_x = (t & 1) == 0
    for j in range(0, rows, 128):
        turned[j : j + 128, :] = a_ref[:, j : j + 128].T
    size = rows // BLOCKS
    for out, order in ((at0_ref, ORDER[0]), (at1_ref, ORDER[1])):
        for p1, e1 in enumerate(order):
            for e2 in range(4):
                block = place ^ jnp.where(along_x, e1 * Y + e2, e2 * Y + e1)
                start = pl.multiple_of(block * size, 16)
                to = (p1 * 4 + e2) * size
                out[to : to + size, :] = turned[pl.ds(start, size), :]


def turn(a):
    tokens, rows = a.shape
    out = [shape(rows, tokens, a.dtype)] * 2
    return local_call(turn_kernel, out, (a,), scratch=[pltpu.VMEM((rows, tokens), a.dtype)])


def exponent_of(bound):
    return jnp.clip(jnp.floor(jnp.log2(HIGH / jnp.maximum(bound, 1e-30))), -60.0, 100.0)


def unit_of(exponent):
    return 1.0 / jnp.exp2(exponent)


def fill(out, at, count, row):
    out[at : at + count, :] = jnp.broadcast_to(row, (count, out.shape[1]))


def squares_kernel(moved, at0, at1, g0, g1, out0, bound0, out1, bound1):
    half, width = at0.shape[0] // 2, g0.shape[1] // 2
    step, base = half // 2, half if moved else 0
    for at, lo, out, bound in ((at0, 0, out0, bound0), (at1, width, out1, bound1)):
        tops = [jnp.zeros((8, width), jnp.float32)] * 2
        for r in range(0, half, step):
            rows = at[base + r : base + r + step, :]
            for h, g in enumerate((g0, g1)):
                grad = jnp.dot(rows, g[:, lo : lo + width], preferred_element_type=jnp.float32)
                grad = grad * grad
                out[r : r + step, h * width : (h + 1) * width] = grad
                tops[h] = jnp.maximum(tops[h], jnp.max(grad.reshape(-1, 8, width), axis=0))
        top = jnp.concatenate([jnp.max(top, axis=0, keepdims=True) for top in tops], axis=1)
        bound[...] = top
        if moved:
            exponent = exponent_of(top)
            scale = jnp.exp2(exponent)
            for r in range(0, half, 80):
                out[r : r + 80, :] = out[r : r + 80, :] * scale
            fill(out, half, TAIL, exponent)


def squares(at0, at1, g0, g1):
    half, width = at0.shape[0] // 2, g0.shape[1]
    both = []
    for moved in (True, False):
        out = [shape(half + TAIL if moved else half, width), shape(1, width)] * 2
        kernel = functools.partial(squares_kernel, moved)
        both.append(local_call(kernel, out, (at0, at1, g0, g1)))
    (out0, _, out1, _), (keep0, bound0, keep1, bound1) = both
    return (keep0, bound0, out0), (keep1, bound1, out1)


def add_kernel(keep0, bound0, got0, keep1, bound1, got1, sum0, top0, sum1, top1):
    rows = keep0.shape[0]
    for keep, bound, got, total, top in (
        (keep0, bound0, got0, sum0, top0),
        (keep1, bound1, got1, sum1, top1),
    ):
        unit = unit_of(got[rows : rows + 1, :])
        top[...] = bound[...] + HIGH * unit
        for r in range(0, rows, 80):
            total[r : r + 80, :] = keep[r : r + 80, :] + got[r : r + 80, :] * unit


def add(*operands):
    rows, width = operands[0].shape
    out = local_call(add_kernel, [shape(rows, width), shape(1, width)] * 2, operands, flops=ADD_COST)
    return out[:2], out[2:]


def halve_kernel(near, near_bound, keep, bound, got, new0, new1, bounds, out):
    rows = keep.shape[0]
    half = rows // 2
    unit = unit_of(got[rows : rows + 1, :])
    tops = (near_bound[...], bound[...] + HIGH * unit)
    exponents = [exponent_of(top) for top in tops]
    scales = [jnp.exp2(exponent) for exponent in exponents]
    for r in range(half, rows, 80):
        to = r - half
        out[to : to + 80, :] = near[r : r + 80, :] * scales[0]
        value = keep[r : r + 80, :] + got[r : r + 80, :] * unit
        out[r : r + 80, :] = value * scales[1]
    for r in range(0, half, 80):
        new0[r : r + 80, :] = near[r : r + 80, :]
        new1[r : r + 80, :] = keep[r : r + 80, :] + got[r : r + 80, :] * unit
    for h in range(2):
        bounds[h : h + 1, :] = tops[h]
        fill(out, rows + h * (TAIL // 2), TAIL // 2, exponents[h])


def halve(*operands):
    rows, width = operands[0].shape
    out = [shape(rows // 2, width)] * 2 + [shape(2, width), shape(rows + TAIL, width)]
    return local_call(halve_kernel, out, operands)


def share_kernel(near0, far0, bounds0, got0, near1, far1, bounds1, got1, own, bounds, *outs):
    rows = near0.shape[0]
    size, each = rows // 4, TAIL // 4
    streams = ((near0, far0, bounds0, got0), (near1, far1, bounds1, got1))
    for s, (near, far, kept_bounds, got) in enumerate(streams):
        for h, keep in enumerate((near, far)):
            p = 2 * s + h
            tail = 2 * rows + h * (TAIL // 2)
            unit = unit_of(got[tail : tail + 1, :])
            top = kept_bounds[h : h + 1, :] + HIGH * unit
            exponent = exponent_of(top)
            scale = jnp.exp2(exponent)
            bounds[p : p + 1, :] = top
            for e, out in ((1, outs[0]), (3, outs[2]), (2, outs[1]), (0, own)):
                at = e * size
                arrived = got[h * rows + at : h * rows + at + size, :]
                value = keep[at : at + size, :] + arrived * unit
                out[p * size : (p + 1) * size, :] = value if e == 0 else value * scale
            for out in outs:
                fill(out, 4 * size + p * each, each, exponent)


def share(*operands):
    rows, width = operands[0].shape
    out = [shape(rows, width), shape(4, width)] + [shape(rows + TAIL, width)] * 3
    own, bounds, *messages = local_call(share_kernel, out, operands)
    return own, bounds, messages


def spread_kernel(own, bounds, got1, got2, got3, *refs):
    outs, staged = refs[:T], refs[T]
    rows, width = own.shape[0], own.shape[1] // 2
    size = rows // 4
    for p in range(4):
        tail = rows + p * (TAIL // 4)
        value, top = own[p * size : (p + 1) * size, :], bounds[p : p + 1, :]
        for got in (got1, got2, got3):
            unit = unit_of(got[tail : tail + 1, :])
            value = value + got[p * size : (p + 1) * size, :] * unit
            top = top + HIGH * unit
        exponent = exponent_of(top)
        value = value * jnp.exp2(exponent)
        s, h = p // 2, p % 2
        for i in range(2):
            q, columns = 2 * h + i, slice(i * width, (i + 1) * width)
            staged[q, s * size : (s + 1) * size, :] = value[:, columns]
            row = jnp.broadcast_to(exponent[:, columns], (TAIL // 2, width))
            to = 2 * size + s * (TAIL // 2)
            staged[q, to : to + TAIL // 2, :] = row
    distance = lax.axis_index("tensor") ^ (lax.axis_index("dp") >> 4)
    for k, out in enumerate(outs):
        out[...] = staged[distance ^ k]


def spread(*operands):
    rows, width = operands[0].shape[0] // 2 + TAIL, operands[0].shape[1] // 2
    scratch = [pltpu.VMEM((T, rows, width), jnp.float32)]
    return local_call(spread_kernel, [shape(rows, width)] * T, operands, scratch=scratch)


def total_kernel(factor, *refs):
    gots, outs = refs[:-2], refs[-2:]
    size = outs[0].shape[0]
    for s, out in enumerate(outs):
        tail = 2 * size + s * (TAIL // 2)
        total = 0.0
        for got in gots:
            unit = factor / jnp.exp2(got[tail : tail + 1, :])
            total = total + got[s * size : (s + 1) * size, :] * unit
        out[...] = total


def total(gots, factor):
    rows, width = (gots[0].shape[0] - TAIL) // 2, gots[0].shape[1]
    return local_call(functools.partial(total_kernel, factor), [shape(rows, width)] * 2, gots)


def right_product(left, right):
    return lax.dot_general(
        left, right, (((1,), (1,)), ((), ())), preferred_element_type=jnp.float32
    )


def narrow(values):
    return [value.astype(jnp.float16) for value in values]


def wide(values):
    return [value.astype(jnp.float32) for value in values]


def per_device(page_acts, out_grad_key, out_grad_value, key_weight, value_weight):
    g0 = join(out_grad_key, out_grad_value)
    g2 = send(g0, tensor_swap(2))
    g1 = send(g0, tensor_swap(1))
    at = turn(page_acts)

    near = squares(*at, g0, g1)
    out = narrow([stream[2] for stream in near])
    near_got = wide([send(out[s], swap(True, FIRST[s])) for s in range(2)])
    kw, vw, _ = lax.optimization_barrier((key_weight, value_weight, out))
    w0, w1, w2, w3 = pick_weights(kw, vw)
    g2, _ = lax.optimization_barrier((g2, w2))
    g3 = send(g2, tensor_swap(1))
    near = add(*near[0][:2], near_got[0], *near[1][:2], near_got[1])
    far = squares(*at, g2, g3)
    out = narrow([stream[2] for stream in far])
    out, near, w2, w3 = lax.optimization_barrier((out, near, w2, w3))
    far_got = [send(out[s], swap(True, FIRST[s])) for s in range(2)]
    w1 = send(w1, tensor_swap(1))
    w1, w2, w3 = lax.optimization_barrier((w1, w2, w3))
    w2 = send(w2, outer_z_swap())
    w3 = send(w3, tensor_swap(3))
    far_got = wide(far_got)

    streams = [halve(*near[s], *far[s][:2], far_got[s]) for s in range(2)]
    out = narrow([stream[3] for stream in streams])
    got = [send(out[s], swap(True, SECOND[s])) for s in range(2)]
    grad_input = right_product(g0, w0) + right_product(g1, w1)
    got, grad_input = lax.optimization_barrier((wide(got), grad_input))
    own, bounds, out = share(*streams[0][:3], got[0], *streams[1][:3], got[1])
    out = narrow(out)
    one, three, two = (send(out[e - 1], swap(False, e)) for e in (1, 3, 2))
    got = [one, two, three]
    got, w2, w3 = lax.optimization_barrier((wide(got), w2, w3))
    outs = spread(own, bounds, *got)
    w1, w2, w3, _ = lax.optimization_barrier((w1, w2, w3, outs))
    got = [send(out, owner_step(k)) for k, out in enumerate(narrow(outs))]
    fisher_key, fisher_value = total(wide(got), 1.0 / (lax.axis_size("dp") * PAGE))

    grad_input = grad_input + (right_product(g2, w2) + right_product(g3, w3))
    return grad_input.astype(jnp.bfloat16), fisher_key, fisher_value


def solution(mesh):
    in_specs = (
        P("dp", "tensor"),
        P("dp", "tensor"),
        P("dp", "tensor"),
        P(None, "tensor"),
        P(None, "tensor"),
    )
    out_specs = (P("dp", "tensor"), P("dp", "tensor"), P("dp", "tensor"))
    return jax.shard_map(
        per_device, mesh=mesh, in_specs=in_specs, out_specs=out_specs, check_vma=False
    )
```
